256 devices in a mesh: tm: 64 (over x, z, core), head: 4 (over y).
Axes of the slice: x: 4, y: 4, z: 8, core: 2. Of those that a mesh axis runs over, the one named last changes fastest.
Arguments:
- queries: bfloat16 [49152, 2560], P(('tm', 'head')), may hold values from -6 to 6
- keys: bfloat16 [49152, 2560], P(('tm', 'head')), may hold values from -6 to 6
- values: bfloat16 [49152, 2560], P(('tm', 'head')), may hold values from -6 to 6
- upstream: bfloat16 [49152, 2560], P(('tm', 'head')), may hold values from -6 to 6
- window: int32 [128, 3], P('tm'), may hold values from -1 to 126, as said below
Outputs:
- grad_queries: bfloat16 [49152, 2560], P(('tm', 'head'))
- grad_keys: bfloat16 [49152, 2560], P(('tm', 'head'))
- grad_values: bfloat16 [49152, 2560], P(('tm', 'head'))
The draws below stay inside these ranges and needn't reach their ends.
Inputs may be any that keep to these rules, and one draw needn't show every extreme that they name: Entry window[c, t] is either c - 1 - t or -1; slot 0 always holds c - 1 (so -1 for group 0).
All inputs are finite; a program needn't handle non-finite values.
Results may differ from the reference program's by a relative error of at most 0.009.
Values may be sent and summed in bfloat16 or wider, within the bound.
No kernel may reach another device: no remote copies, remote signals or barrier semaphores. Data moves between devices by JAX's collectives and lax.ppermute only.
A program may use at most 128 MiB of HBM per device.

```python
import jax
import jax.numpy as jnp
from jax import lax

CT = 384
SPAN = 3
HEADS = 20
HD = 128
GROUPS = 128
TOKENS = 49152


def draw_queries(key, part):
    key = jax.random.fold_in(key, 11)
    base = jax.random.normal(key, (TOKENS, HEADS * HD), jnp.float32)
    return jnp.clip(base, -6.0, 6.0).astype(jnp.bfloat16)


def draw_keys(key, part):
    key = jax.random.fold_in(key, 12)
    base = jax.random.normal(key, (TOKENS, HEADS * HD), jnp.float32)
    return jnp.clip(base, -6.0, 6.0).astype(jnp.bfloat16)


def draw_window(key, part):
    key = jax.random.fold_in(key, 13)
    group_ids = jnp.arange(GROUPS, dtype=jnp.int32)[:, None]
    slot_ids = jnp.arange(SPAN, dtype=jnp.int32)[None, :]
    listed = group_ids - 1 - slot_ids
    keeping = jax.random.randint(key, (GROUPS, SPAN), 0, 2)
    keeping = jnp.where(slot_ids == 0, 1, keeping)
    return jnp.where((keeping == 1) & (listed >= 0), listed, -1).astype(jnp.int32)


def steps_of(stream_key, shape, shards, smallest, largest):
    gain, own = 1.0, jax.random.fold_in(stream_key, 6)
    for dim, blocks in shards:
        draws = jnp.exp(jax.random.uniform(jax.random.fold_in(own, dim), (blocks,), jnp.float32, smallest / len(shards), largest / len(shards)))
        gain = gain * jnp.repeat(draws, shape[dim] // blocks).reshape([-1 if axis == dim else 1 for axis in range(len(shape))])
    return gain


def scatter_about(key, extent, deviation, most, shards=(), kind=jnp.bfloat16):
    array = jax.random.normal(key, extent, jnp.float32) * deviation
    if len(shards) > 0:
        array = steps_of(key, extent, shards, -0.22, 0.18) * array
    return jnp.clip(array, min=-most, max=most).astype(kind)


def setup_inputs(seed: int = 0) -> dict:
    key_of = jax.random.split(jax.random.key(seed), 6)
    queries = draw_queries(jax.random.fold_in(key_of[5], 71), 0)
    keys = draw_keys(jax.random.fold_in(key_of[5], 71), 0)
    values = scatter_about(key_of[2], (TOKENS, HEADS * HD), 1.0, 6.0, ((0, 256),))
    upstream = scatter_about(key_of[3], (TOKENS, HEADS * HD), 1.0, 6.0, ((0, 256),))
    window = draw_window(jax.random.fold_in(key_of[5], 71), 0)
    return dict(queries=queries, keys=keys, values=values, upstream=upstream, window=window)


def reference(queries, keys, values, upstream, window):
    score_scale = 1.0 / (HD ** 0.5)
    col_count = HEADS * HD
    span_rows = (SPAN + 1) * CT
    padding = jnp.zeros((SPAN * CT, col_count), keys.dtype)
    keys_pad = jnp.concatenate([padding, keys], 0)
    values_pad = jnp.concatenate([padding, values], 0)
    offsets = jnp.arange(SPAN + 1, dtype=jnp.int32)

    def step(carry, index):
        grad_k, grad_v = carry
        start = (index * CT).astype(jnp.int32)
        q_rows = lax.dynamic_slice_in_dim(queries, start, CT, 0).reshape(CT, HEADS, HD).astype(jnp.float32)
        g_rows = lax.dynamic_slice_in_dim(upstream, start, CT, 0).reshape(CT, HEADS, HD).astype(jnp.float32)
        k_rows = lax.dynamic_slice_in_dim(keys_pad, start, span_rows, 0).reshape(span_rows, HEADS, HD).astype(jnp.float32)
        v_rows = lax.dynamic_slice_in_dim(values_pad, start, span_rows, 0).reshape(span_rows, HEADS, HD).astype(jnp.float32)
        listed = lax.dynamic_slice_in_dim(window, index, 1, 0)[0]
        group_ids = index - SPAN + offsets
        seen = (group_ids == index) | (jnp.any(listed[None, :] == group_ids[:, None], axis=1) & (group_ids >= 0))
        allowed = jnp.repeat(seen, CT)
        scores = jnp.einsum("qhd,khd->hqk", q_rows, k_rows) * score_scale
        scores = jnp.where(allowed[None, None, :], scores, -1e30)
        row_top = jnp.max(scores, axis=2, keepdims=True)
        weights = jnp.exp(scores - row_top)
        probs = weights / jnp.sum(weights, axis=2, keepdims=True)
        probs_b = lax.optimization_barrier(probs.astype(jnp.bfloat16)).astype(jnp.float32)
        output = jnp.einsum("hqk,khd->qhd", probs_b, v_rows)
        delta = jnp.sum(g_rows * output, axis=2)
        dprobs = jnp.einsum("qhd,khd->hqk", g_rows, v_rows)
        dscores = probs * (dprobs - jnp.transpose(delta)[:, :, None])
        dscores_b = lax.optimization_barrier(dscores.astype(jnp.bfloat16)).astype(jnp.float32)
        grad_q = jnp.einsum("hqk,khd->qhd", dscores_b, k_rows) * score_scale
        part_k = (jnp.einsum("hqk,qhd->khd", dscores_b, q_rows) * score_scale).reshape(span_rows, col_count)
        part_v = jnp.einsum("hqk,qhd->khd", probs_b, g_rows).reshape(span_rows, col_count)
        old_k = lax.dynamic_slice_in_dim(grad_k, start, span_rows, 0)
        old_v = lax.dynamic_slice_in_dim(grad_v, start, span_rows, 0)
        grad_k = lax.dynamic_update_slice_in_dim(grad_k, old_k + part_k, start, 0)
        grad_v = lax.dynamic_update_slice_in_dim(grad_v, old_v + part_v, start, 0)
        return (grad_k, grad_v), grad_q.reshape(CT, col_count).astype(jnp.bfloat16)

    zeros_init = jnp.zeros(((GROUPS + SPAN) * CT, col_count), jnp.float32)
    (grad_k, grad_v), grad_q = lax.scan(step, (zeros_init, zeros_init), jnp.arange(GROUPS, dtype=jnp.int32))
    grad_queries = grad_q.reshape(TOKENS, col_count)
    grad_keys = grad_k[SPAN * CT:].astype(jnp.bfloat16)
    grad_values = grad_v[SPAN * CT:].astype(jnp.bfloat16)
    return (grad_queries, grad_keys, grad_values)
```

```python
import functools
import math

import jax
import jax.numpy as jnp
from jax import lax
from jax.experimental import pallas as pl
from jax.experimental.pallas import tpu as pltpu
from jax.sharding import PartitionSpec as P

HD = 128
GR = 384
PR = 192
HEADS_DEV = 5
CHUNKS = (2, 2, 1)
SCALE = 1.0 / math.sqrt(HD)
SCALE2 = SCALE * math.log2(math.e)
NT = (((1,), (1,)), ((), ()))
TN = (((0,), (0,)), ((), ()))
BF = jnp.bfloat16
F32 = jnp.float32
VM = pl.BlockSpec(memory_space=pltpu.VMEM)


def dot(a, b, dims=(((1,), (0,)), ((), ()))):
    return lax.dot_general(a, b, dims, preferred_element_type=F32)


def cost(flops, nbytes):
    return pl.CostEstimate(flops=int(flops), bytes_accessed=int(nbytes), transcendentals=0)


def head_shift(block, distance):
    n = lax.axis_size("head")
    return lax.ppermute(block, "head", [(i, (i + distance) % n) for i in range(n)])


def tm_shift(block, distance):
    devices = range(lax.axis_size("tm"))
    route = [(i - distance, i) for i in devices if i - distance in devices]
    return lax.ppermute(block, "tm", route)


def head_columns(owner, off, w):
    return pl.ds(pl.multiple_of(owner * (HEADS_DEV * HD) + off, HD), w)


def piece_rows(owner):
    return pl.ds(pl.multiple_of(owner * PR, 64), PR)


def pack_kernel(offsets, k, v, q, g, *outs):
    me = lax.axis_index("head")
    for c, (off, w) in enumerate(offsets):
        for d, out in zip((1, 3, 2), outs[3 * c : 3 * c + 3]):
            cols = head_columns(lax.rem(me + d, 4), off, w)
            for i, src in enumerate((k, v, q, g)):
                out[i] = src[:, cols]


def pack(k, v, q, g, offsets):
    outs = [jax.ShapeDtypeStruct((4, PR, w), BF) for _, w in offsets for _ in range(3)]
    return pl.pallas_call(
        functools.partial(pack_kernel, offsets),
        in_specs=[VM] * 4,
        out_specs=[VM] * len(outs),
        out_shape=outs,
        compiler_params=pltpu.CompilerParams(vmem_limit_bytes=40 << 20),
        cost_estimate=cost(0, 24 * PR * 640 * 2),
        name="pack",
    )(k, v, q, g)


def join_kernel(off, w, k, v, r1, r2, r3, own, last):
    me = lax.axis_index("head")
    cols = head_columns(me, off, w)
    own[0, piece_rows(me), :] = k[:, cols]
    own[1, piece_rows(me), :] = v[:, cols]
    for d, r in ((1, r1), (3, r2), (2, r3)):
        rows = piece_rows(lax.rem(me + 4 - d, 4))
        own[0, rows, :] = r[0]
        own[1, rows, :] = r[1]
    last[...] = own[:, GR:, :]


def join(k, v, r, off, w):
    return pl.pallas_call(
        functools.partial(join_kernel, off, w),
        in_specs=[VM] * 5,
        out_specs=[VM] * 2,
        out_shape=[
            jax.ShapeDtypeStruct((2, 2 * GR, w), BF),
            jax.ShapeDtypeStruct((2, GR, w), BF),
        ],
        compiler_params=pltpu.CompilerParams(vmem_limit_bytes=40 << 20),
        cost_estimate=cost(0, 6 * 2 * GR * w * 2),
        name="join",
    )(k, v, *r)


def attend_kernel(
    win, me_ref, near, far, own, q0, g0, r1, r2, r3,
    dq_ref, nearg, farg, owng, q_ref, g_ref, s_ref, d_ref,
):
    me = me_ref[0]
    q_ref[piece_rows(me), :] = q0[...]
    g_ref[piece_rows(me), :] = g0[...]
    for d, r in ((1, r1), (3, r2), (2, r3)):
        rows = piece_rows(lax.rem(me + 4 - d, 4))
        q_ref[rows, :] = r[0]
        g_ref[rows, :] = r[1]
    q = q_ref[...]
    g = g_ref[...]

    def hidden(c, slot):
        return jnp.where(win[c, slot] >= 0, 0.0, 1e30).astype(F32)

    lane = lax.broadcasted_iota(jnp.int32, (1, 2 * GR), 1)

    def lanes(a, b):
        return jnp.where(lane < GR, a, b)

    blocks = (
        (far, farg, 0, 0, 0, GR, jnp.full((1, GR), 1.0, F32) * hidden(0, 2)),
        (near, nearg, 0, 1, 0, 2 * GR, lanes(hidden(0, 1), hidden(1, 2))),
        (near, nearg, 1, 2, 0, 2 * GR, lanes(hidden(0, 0), hidden(1, 1))),
        (own, owng, 0, 3, 0, 2 * GR, lanes(0.0, hidden(1, 0))),
        (own, owng, 1, 4, GR, 2 * GR, jnp.zeros((1, GR), F32)),
    )

    def rows_of(i):
        return slice(i * GR, (i + 1) * GR)

    def combine(x, op):
        mid = op(op(x[1], x[2]), x[3])
        return jnp.concatenate([op(mid[:, :GR], x[0]), op(mid[:, GR:], x[4])], axis=1)

    tops = []
    for ref, _, i, j, lo, hi, hide in blocks:
        s = dot(ref[0, rows_of(i), :], q[lo:hi], NT)
        s_ref[rows_of(j), lo:hi] = s
        tops.append(jnp.max(s, axis=0, keepdims=True) * SCALE2 - hide)
    top = combine(tops, jnp.maximum)
    totals, deltas = [], []
    for ref, _, i, j, lo, hi, hide in blocks:
        dp = dot(ref[1, rows_of(i), :], g[lo:hi], NT)
        e = jnp.exp2(s_ref[rows_of(j), lo:hi] * SCALE2 - (top[:, lo:hi] + hide))
        s_ref[rows_of(j), lo:hi] = e
        d_ref[rows_of(j), lo:hi] = dp
        totals.append(jnp.sum(e, axis=0, keepdims=True))
        deltas.append(jnp.sum(e * dp, axis=0, keepdims=True))
    inverse = 1.0 / combine(totals, jnp.add)
    delta = combine(deltas, jnp.add) * inverse
    dq = [None, None]
    for ref, out, i, j, lo, hi, hide in blocks:
        p = s_ref[rows_of(j), lo:hi] * inverse[:, lo:hi]
        ds = (p * (d_ref[rows_of(j), lo:hi] - delta[:, lo:hi])).astype(BF)
        out[1, rows_of(i), :] = dot(p.astype(BF), g[lo:hi]).astype(out.dtype)
        out[0, rows_of(i), :] = (dot(ds, q[lo:hi]) * SCALE).astype(out.dtype)
        part = dot(ref[0, rows_of(i), :], ds, TN)
        if lo == 0:
            dq[0] = part[:, :GR] if dq[0] is None else dq[0] + part[:, :GR]
        if hi == 2 * GR:
            dq[1] = part[:, -GR:] if dq[1] is None else dq[1] + part[:, -GR:]
    for i in range(2):
        dq_ref[rows_of(i), :] = (dq[i].T * SCALE).astype(BF)


def attend(window, me, near, far, own, q, g, r, off, w):
    heads = w // HD

    def three(a, rows, first=0):
        return pl.BlockSpec((a, rows, HD), lambda h, win, m: (first, 0, h))

    def flat(rows):
        return pl.BlockSpec((rows, HD), lambda h, win, m: (0, h))

    mine = pl.BlockSpec((PR, HD), lambda h, win, m: (0, m[0] * HEADS_DEV + off // HD + h))
    sd = jax.ShapeDtypeStruct
    return pl.pallas_call(
        attend_kernel,
        grid_spec=pltpu.PrefetchScalarGridSpec(
            num_scalar_prefetch=2,
            grid=(heads,),
            in_specs=[three(2, 2 * GR), three(2, GR), three(2, 2 * GR), mine, mine]
            + [three(2, PR, 1)] * 3,
            out_specs=[flat(2 * GR), three(2, 2 * GR), three(2, GR), three(2, 2 * GR)],
            scratch_shapes=[
                pltpu.VMEM((2 * GR, HD), BF),
                pltpu.VMEM((2 * GR, HD), BF),
                pltpu.VMEM((5 * GR, 2 * GR), F32),
                pltpu.VMEM((5 * GR, 2 * GR), F32),
            ],
        ),
        out_shape=[
            sd((2 * GR, w), BF),
            sd((2, 2 * GR, w), BF),
            sd((2, GR, w), BF),
            sd((2, 2 * GR, w), F32),
        ],
        compiler_params=pltpu.CompilerParams(vmem_limit_bytes=40 << 20),
        cost_estimate=cost(heads * 5.5e9, heads * 3e6),
        name="attend",
    )(window, me, near, far, own, q, g, *r)


def settle_kernel(me_ref, dq, owng, nearg, farg, o0, o1, o2, o3):
    me = me_ref[0]
    for d, out in ((0, o0), (1, o1), (3, o2), (2, o3)):
        owner = lax.rem(me + d, 4)
        rows = piece_rows(owner)
        far_rows = piece_rows(lax.rem(owner, 2))
        out[0] = dq[rows, :]
        for i in range(2):
            late = jnp.where(owner >= 2, farg[i, far_rows, :].astype(F32), 0.0)
            out[1 + i] = (owng[i, rows, :] + nearg[i, rows, :].astype(F32) + late).astype(BF)


def settle(me, dq, owng, nearg, farg, w):
    def three(a, rows):
        return pl.BlockSpec((a, rows, HD), lambda h, m: (0, 0, h))

    return pl.pallas_call(
        settle_kernel,
        grid_spec=pltpu.PrefetchScalarGridSpec(
            num_scalar_prefetch=1,
            grid=(w // HD,),
            in_specs=[
                pl.BlockSpec((2 * GR, HD), lambda h, m: (0, h)),
                three(2, 2 * GR),
                three(2, 2 * GR),
                three(2, GR),
            ],
            out_specs=[three(3, PR)] * 4,
        ),
        out_shape=[jax.ShapeDtypeStruct((3, PR, w), BF)] * 4,
        cost_estimate=cost(0, 10 * 2 * GR * w * 2),
        name="settle",
    )(me, dq, owng, nearg, farg)


def place_kernel(offsets, *refs):
    n = len(offsets)
    outs = refs[4 * n :]
    me = lax.axis_index("head")
    for c, (off, w) in enumerate(offsets):
        for d, r in zip((0, 1, 3, 2), refs[4 * c : 4 * c + 4]):
            cols = head_columns(lax.rem(me + 4 - d, 4), off, w)
            for i in range(3):
                outs[i][:, cols] = r[i]


def place(offsets, pieces):
    out = jax.ShapeDtypeStruct((PR, 4 * HEADS_DEV * HD), BF)
    n = len(pieces)
    return pl.pallas_call(
        functools.partial(place_kernel, offsets),
        in_specs=[VM] * n,
        out_specs=[VM] * 3,
        out_shape=[out] * 3,
        compiler_params=pltpu.CompilerParams(vmem_limit_bytes=40 << 20),
        cost_estimate=cost(0, 6 * PR * 2560 * 2),
        name="place",
    )(*pieces)


def shift_all(pieces):
    a, b, c = pieces
    return head_shift(a, 1), head_shift(b, -1), head_shift(c, 2)


def local(queries, keys, values, upstream, window):
    me = lax.axis_index("head").astype(jnp.int32).reshape(1)
    offsets = []
    off = 0
    for heads in CHUNKS:
        offsets.append((off, heads * HD))
        off += heads * HD
    offsets = tuple(offsets)
    packed = pack(keys, values, queries, upstream, offsets)
    came = [shift_all(packed[3 * c : 3 * c + 3]) for c in range(len(offsets))]
    pieces = []
    for (off, w), r in zip(offsets, came):
        own, last = join(keys, values, r, off, w)
        near = tm_shift(own, 1)
        far = tm_shift(last, 2)
        dq, nearg, farg, owng = attend(
            window, me, near, far, own, queries, upstream, r, off, w
        )
        back_near = tm_shift(nearg, -1)
        back_far = tm_shift(farg, -2)
        o0, *parts = settle(me, dq, owng, back_near, back_far, w)
        pieces += [o0, *shift_all(parts)]
    return place(offsets, pieces)


def solution(mesh):
    rows = P(("tm", "head"), None)
    return jax.shard_map(
        local,
        mesh=mesh,
        in_specs=(rows, rows, rows, rows, P("tm", None)),
        out_specs=(rows, rows, rows),
        check_vma=False,
    )
```

```python
import functools
import math

import jax
import jax.numpy as jnp
from jax import lax
from jax.experimental import pallas as pl
from jax.experimental.pallas import tpu as pltpu
from jax.sharding import PartitionSpec as P

HD = 128
GR = 384
PR = 192
HEADS_DEV = 5
CHUNKS = (2, 3)
IN_STAGES = (
    (("kv", 0),),
    (("qg", 0), ("kv", 1)),
    (("qg", 1),),
)
OUT_STAGES = ((("dq", 0), ("dkv", 0), ("dq", 1)), (("dkv", 1),))
SCALE = 1.0 / math.sqrt(HD)
SCALE2 = SCALE * math.log2(math.e)
NT = (((1,), (1,)), ((), ()))
TN = (((0,), (0,)), ((), ()))
BF = jnp.bfloat16
F32 = jnp.float32
VM = pl.BlockSpec(memory_space=pltpu.VMEM)


def dot(a, b, dims=(((1,), (0,)), ((), ()))):
    return lax.dot_general(a, b, dims, preferred_element_type=F32)


def cost(flops, nbytes):
    return pl.CostEstimate(flops=int(flops * 1), bytes_accessed=int(nbytes * 1), transcendentals=0)


def head_shift(block, distance):
    n = lax.axis_size("head")
    return lax.ppermute(block, "head", [(i, (i + distance) % n) for i in range(n)])


def tm_shift(block, distance):
    devices = range(lax.axis_size("tm"))
    route = [(i - distance, i) for i in devices if i - distance in devices]
    return lax.ppermute(block, "tm", route)


def columns(owner, head):
    return pl.ds(pl.multiple_of((owner * HEADS_DEV + head) * HD, HD), HD)


def piece_rows(owner):
    return pl.ds(pl.multiple_of(owner * PR, 64), PR)


def heads_of(chunk):
    first = sum(CHUNKS[:chunk])
    return range(first, first + CHUNKS[chunk])


def in_units(stage):
    units = []
    for what, chunk in stage:
        for head in heads_of(chunk):
            units += [(what[0], head), (what[1], head)]
    return units


def out_units(stage):
    units = []
    for what, chunk in stage:
        for head in heads_of(chunk):
            units += [(o, head) for o in what[1:]]
    return units


def small():
    return pltpu.CompilerParams(vmem_limit_bytes=24 << 20)


def pack_kernel(units, names, *refs):
    me = lax.axis_index("head")
    srcs = dict(zip(names, refs))
    for d, out in zip((1, 3, 2), refs[len(names) :]):
        owner = lax.rem(me + d, 4)
        for u, (name, head) in enumerate(units):
            out[u] = srcs[name][:, columns(owner, head)]


def pack(args, stage):
    units = in_units(stage)
    names = sorted({name for name, _ in units})
    out = jax.ShapeDtypeStruct((len(units), PR, HD), BF)
    return pl.pallas_call(
        functools.partial(pack_kernel, units, names),
        in_specs=[VM] * len(names),
        out_specs=[VM] * 3,
        out_shape=[out] * 3,
        compiler_params=small(),
        cost_estimate=cost(0, 6 * len(units) * PR * HD * 2),
        name="pack",
    )(*[args[name] for name in names])


def join_kernel(heads, base, k, v, r1, r2, r3, own, last):
    me = lax.axis_index("head")
    for n, head in enumerate(heads):
        own[n, 0, piece_rows(me), :] = k[:, columns(me, head)]
        own[n, 1, piece_rows(me), :] = v[:, columns(me, head)]
        for d, r in ((1, r1), (3, r2), (2, r3)):
            rows = piece_rows(lax.rem(me + 4 - d, 4))
            own[n, 0, rows, :] = r[base + 2 * n]
            own[n, 1, rows, :] = r[base + 2 * n + 1]
    last[...] = own[:, :, GR:, :]


def join(k, v, r, heads, base):
    n = len(heads)
    return pl.pallas_call(
        functools.partial(join_kernel, heads, base),
        in_specs=[VM] * 5,
        out_specs=[VM] * 2,
        out_shape=[
            jax.ShapeDtypeStruct((n, 2, 2 * GR, HD), BF),
            jax.ShapeDtypeStruct((n, 2, GR, HD), BF),
        ],
        compiler_params=small(),
        cost_estimate=cost(0, 6 * 2 * GR * n * HD * 2),
        name="join",
    )(k, v, *r)


def attend_kernel(
    heads, base, win, near_, far_, own_, queries, upstream, r1, r2, r3,
    dq_, nearg_, farg_, owng_, q_ref, g_ref, s_ref, d_ref,
):
    me = lax.axis_index("head")

    def hidden(c, slot):
        return jnp.where(win[c, slot] >= 0, 0.0, 1e30).astype(F32)

    lane = lax.broadcasted_iota(jnp.int32, (1, 2 * GR), 1)

    def lanes(a, b):
        return jnp.where(lane < GR, a, b)

    one = jnp.full((1, GR), 1.0, F32)
    hides = (
        one * hidden(0, 2),
        lanes(hidden(0, 1), hidden(1, 2)),
        lanes(hidden(0, 0), hidden(1, 1)),
        lanes(0.0, hidden(1, 0)),
        one * 0.0,
    )

    def rows_of(i):
        return slice(i * GR, (i + 1) * GR)

    def combine(x, op):
        mid = op(op(x[1], x[2]), x[3])
        return jnp.concatenate([op(mid[:, :GR], x[0]), op(mid[:, GR:], x[4])], axis=1)

    def head(n, carry):
        near, far, own = near_.at[n], far_.at[n], own_.at[n]
        nearg, farg, owng = nearg_.at[n], farg_.at[n], owng_.at[n]
        q_ref[piece_rows(me), :] = queries[:, columns(me, heads[0] + n)]
        g_ref[piece_rows(me), :] = upstream[:, columns(me, heads[0] + n)]
        for d, r in ((1, r1), (3, r2), (2, r3)):
            rows = piece_rows(lax.rem(me + 4 - d, 4))
            q_ref[rows, :] = r[base + 2 * n]
            g_ref[rows, :] = r[base + 2 * n + 1]
        blocks = (
            (far, farg, 0, 0, 0, GR, hides[0]),
            (near, nearg, 0, 1, 0, 2 * GR, hides[1]),
            (near, nearg, 1, 2, 0, 2 * GR, hides[2]),
            (own, owng, 0, 3, 0, 2 * GR, hides[3]),
            (own, owng, 1, 4, GR, 2 * GR, hides[4]),
        )
        tops = []
        for ref, _, i, j, lo, hi, hide in blocks:
            s = dot(ref[0, rows_of(i), :], q_ref[lo:hi, :], NT)
            s_ref[rows_of(j), lo:hi] = s
            tops.append(jnp.max(s, axis=0, keepdims=True) * SCALE2 - hide)
        top = combine(tops, jnp.maximum)
        totals, deltas = [], []
        for ref, _, i, j, lo, hi, hide in blocks:
            dp = dot(ref[1, rows_of(i), :], g_ref[lo:hi, :], NT)
            e = jnp.exp2(s_ref[rows_of(j), lo:hi] * SCALE2 - (top[:, lo:hi] + hide))
            s_ref[rows_of(j), lo:hi] = e
            d_ref[rows_of(j), lo:hi] = dp
            totals.append(jnp.sum(e, axis=0, keepdims=True))
            deltas.append(jnp.sum(e * dp, axis=0, keepdims=True))
        inverse = 1.0 / combine(totals, jnp.add)
        delta = combine(deltas, jnp.add) * inverse
        column = jnp.transpose(jnp.broadcast_to(inverse, (HD, 2 * GR)))
        g = (g_ref[...].astype(F32) * column).astype(BF)
        q = (q_ref[...].astype(F32) * (column * SCALE)).astype(BF)
        dq = [None, None]
        for ref, out, i, j, lo, hi, hide in blocks:
            e = s_ref[rows_of(j), lo:hi]
            ds = (e * (d_ref[rows_of(j), lo:hi] - delta[:, lo:hi])).astype(BF)
            out[1, rows_of(i), :] = dot(e.astype(BF), g[lo:hi]).astype(out.dtype)
            out[0, rows_of(i), :] = dot(ds, q[lo:hi]).astype(out.dtype)
            part = dot(ref[0, rows_of(i), :], ds, TN)
            if lo == 0:
                dq[0] = part[:, :GR] if dq[0] is None else dq[0] + part[:, :GR]
            if hi == 2 * GR:
                dq[1] = part[:, -GR:] if dq[1] is None else dq[1] + part[:, -GR:]
        for i in range(2):
            factor = inverse[:, rows_of(i)] * SCALE
            dq_[n, rows_of(i), :] = (dq[i] * factor).T.astype(BF)
        return carry

    if len(heads) == 1:
        head(0, 0)
    else:
        lax.fori_loop(0, len(heads), head, 0)


def attend(window, near, far, own, queries, upstream, r, heads, base):
    n = len(heads)
    sd = jax.ShapeDtypeStruct
    return pl.pallas_call(
        functools.partial(attend_kernel, heads, base),
        in_specs=[pl.BlockSpec(memory_space=pltpu.SMEM)] + [VM] * 8,
        out_specs=[VM] * 4,
        out_shape=[
            sd((n, 2 * GR, HD), BF),
            sd((n, 2, 2 * GR, HD), BF),
            sd((n, 2, GR, HD), BF),
            sd((n, 2, 2 * GR, HD), F32),
        ],
        scratch_shapes=[
            pltpu.VMEM((2 * GR, HD), BF),
            pltpu.VMEM((2 * GR, HD), BF),
            pltpu.VMEM((5 * GR, 2 * GR), F32),
            pltpu.VMEM((5 * GR, 2 * GR), F32),
        ],
        compiler_params=pltpu.CompilerParams(vmem_limit_bytes=32 << 20),
        cost_estimate=cost(n * 5.5e9, n * 3e6),
        name="attend",
    )(window, near, far, own, queries, upstream, *r)


def settle_kernel(stage, *refs):
    me = lax.axis_index("head")
    outs = refs[-4:]
    refs = list(refs[:-4])
    u = 0
    for what, chunk in stage:
        if what == "dq":
            dq = refs.pop(0)
        else:
            owng, nearg, farg = refs.pop(0), refs.pop(0), refs.pop(0)
        for n in range(CHUNKS[chunk]):
            for d, out in zip((0, 1, 3, 2), outs):
                owner = lax.rem(me + d, 4)
                rows = piece_rows(owner)
                far_rows = piece_rows(lax.rem(owner, 2))
                if what == "dq":
                    out[u] = dq[n, rows, :]
                    continue
                for i in range(2):
                    late = jnp.where(owner >= 2, farg[n, i, far_rows, :].astype(F32), 0.0)
                    total = owng[n, i, rows, :] + nearg[n, i, rows, :].astype(F32) + late
                    out[u + i] = total.astype(BF)
            u += 1 if what == "dq" else 2


def settle(stage, operands):
    out = jax.ShapeDtypeStruct((len(out_units(stage)), PR, HD), BF)
    return pl.pallas_call(
        functools.partial(settle_kernel, stage),
        in_specs=[VM] * len(operands),
        out_specs=[VM] * 4,
        out_shape=[out] * 4,
        compiler_params=small(),
        cost_estimate=cost(0, 16 * len(out_units(stage)) * PR * HD * 2),
        name="settle",
    )(*operands)


def place_kernel(*refs):
    outs = dict(zip("qkv", refs[-3:]))
    me = lax.axis_index("head")
    for c, stage in enumerate(OUT_STAGES):
        for d, r in zip((0, 1, 3, 2), refs[4 * c : 4 * c + 4]):
            owner = lax.rem(me + 4 - d, 4)
            for u, (name, head) in enumerate(out_units(stage)):
                outs[name][:, columns(owner, head)] = r[u]


def place(pieces):
    out = jax.ShapeDtypeStruct((PR, 4 * HEADS_DEV * HD), BF)
    n = len(pieces)
    return pl.pallas_call(
        place_kernel,
        in_specs=[VM] * n,
        out_specs=[VM] * 3,
        out_shape=[out] * 3,
        compiler_params=small(),
        cost_estimate=cost(0, 6 * PR * 2560 * 2),
        name="place",
    )(*pieces)


def shift_all(pieces):
    a, b, c = pieces
    c = head_shift(c, 2)
    return head_shift(a, 1), head_shift(b, -1), c


def after(x, earlier):
    return lax.optimization_barrier((x, earlier))[0]


def local(queries, keys, values, upstream, window):
    args = {"q": queries, "k": keys, "v": values, "g": upstream}
    place_of = {}
    for i, stage in enumerate(IN_STAGES):
        base = 0
        for what, chunk in stage:
            place_of[what, chunk] = (i, base)
            base += 2 * CHUNKS[chunk]
    packed = [pack(args, stage) for stage in IN_STAGES]
    came = {}
    local_of = {}
    other = {}
    back = {}

    def send_in(i):
        came[i] = shift_all(packed[i])

    def join_chunk(c):
        i, base = place_of["kv", c]
        local_of[c] = join(keys, values, came[i], heads_of(c), base)

    def send_near(c):
        own, last = local_of[c]
        other[c] = tm_shift(own, 1), tm_shift(last, 2)

    def attend_chunk(c):
        i, base = place_of["qg", c]
        return attend(
            window, *other[c], local_of[c][0], queries, upstream, came[i], heads_of(c), base
        )

    def send_back(c):
        back[c] = tm_shift(grads[c][1], -1), tm_shift(grads[c][2], -2)

    grads = {}
    pieces = {}
    kept = {}

    def settle_stage(j):
        operands = []
        for what, c in OUT_STAGES[j]:
            operands += [grads[c][0]] if what == "dq" else [grads[c][3], *back[c]]
        own, *parts = settle(OUT_STAGES[j], operands)
        kept[j] = own
        return parts

    def send_out(j, parts):
        pieces[j] = [kept[j], *shift_all(parts)]

    send_in(0)
    send_in(1)
    join_chunk(0)
    send_near(0)
    join_chunk(1)
    local_of[1] = after(local_of[1], other[0])
    send_near(1)
    packed[2] = after(packed[2], local_of[1])
    send_in(2)
    grads[0] = attend_chunk(0)
    came[2] = after(came[2], grads[0][0])
    send_back(0)
    grads[1] = attend_chunk(1)
    grads[1] = after(grads[1], back[0])
    parts0 = settle_stage(0)
    send_out(0, parts0)
    send_back(1)
    parts1 = settle_stage(1)
    parts1 = [after(x, y) for x, y in zip(parts1, pieces[0][1:])]
    send_out(1, parts1)
    return place([x for j in range(2) for x in pieces[j]])


def solution(mesh):
    rows = P(("tm", "head"), None)
    return jax.shard_map(
        local,
        mesh=mesh,
        in_specs=(rows, rows, rows, rows, P("tm", None)),
        out_specs=(rows, rows, rows),
        check_vma=False,
    )
```

```python
import functools
import math

import jax
import jax.numpy as jnp
from jax import lax
from jax.experimental import pallas as pl
from jax.experimental.pallas import tpu as pltpu
from jax.sharding import PartitionSpec as P

HD = 128
GR = 384
PR = 192
HEADS_DEV = 5
CHUNKS = (2, 3)
IN_STAGES = (
    (("kv", 0),),
    (("qg", 0), ("kv", 1)),
    (("qg", 1),),
)
OUT_STAGES = ((("dq", 0), ("dkv", 0), ("dq", 1)), (("dkv", 1),))
SCALE = 1.0 / math.sqrt(HD)
SCALE2 = SCALE * math.log2(math.e)
NT = (((1,), (1,)), ((), ()))
TN = (((0,), (0,)), ((), ()))
BF = jnp.bfloat16
F32 = jnp.float32
VM = pl.BlockSpec(memory_space=pltpu.VMEM)


def dot(a, b, dims=(((1,), (0,)), ((), ()))):
    return lax.dot_general(a, b, dims, preferred_element_type=F32)


def cost(flops, nbytes):
    return pl.CostEstimate(flops=int(flops * 1), bytes_accessed=int(nbytes * 1), transcendentals=0)


def head_shift(block, distance):
    n = lax.axis_size("head")
    return lax.ppermute(block, "head", [(i, (i + distance) % n) for i in range(n)])


def tm_shift(block, distance):
    devices = range(lax.axis_size("tm"))
    route = [(i - distance, i) for i in devices if i - distance in devices]
    return lax.ppermute(block, "tm", route)


def columns(owner, head):
    return pl.ds(pl.multiple_of((owner * HEADS_DEV + head) * HD, HD), HD)


def piece_rows(owner):
    return pl.ds(pl.multiple_of(owner * PR, 64), PR)


def heads_of(chunk):
    first = sum(CHUNKS[:chunk])
    return range(first, first + CHUNKS[chunk])


def in_units(stage):
    units = []
    for what, chunk in stage:
        for head in heads_of(chunk):
            units += [(what[0], head), (what[1], head)]
    return units


def out_units(stage):
    units = []
    for what, chunk in stage:
        for head in heads_of(chunk):
            units += [(o, head) for o in what[1:]]
    return units


def small():
    return pltpu.CompilerParams(vmem_limit_bytes=24 << 20)


def pack_kernel(units, names, *refs):
    me = lax.axis_index("head")
    srcs = dict(zip(names, refs))
    for d, out in zip((1, 3, 2), refs[len(names) :]):
        owner = lax.rem(me + d, 4)
        for u, (name, head) in enumerate(units):
            out[u] = srcs[name][:, columns(owner, head)]


def pack(args, stage):
    units = in_units(stage)
    names = sorted({name for name, _ in units})
    out = jax.ShapeDtypeStruct((len(units), PR, HD), BF)
    return pl.pallas_call(
        functools.partial(pack_kernel, units, names),
        in_specs=[VM] * len(names),
        out_specs=[VM] * 3,
        out_shape=[out] * 3,
        compiler_params=small(),
        cost_estimate=cost(0, 6 * len(units) * PR * HD * 2),
        name="pack",
    )(*[args[name] for name in names])


def join_kernel(heads, base, k, v, r1, r2, r3, own, last):
    me = lax.axis_index("head")
    for n, head in enumerate(heads):
        own[n, 0, piece_rows(me), :] = k[:, columns(me, head)]
        own[n, 1, piece_rows(me), :] = v[:, columns(me, head)]
        for d, r in ((1, r1), (3, r2), (2, r3)):
            rows = piece_rows(lax.rem(me + 4 - d, 4))
            own[n, 0, rows, :] = r[base + 2 * n]
            own[n, 1, rows, :] = r[base + 2 * n + 1]
    last[...] = own[:, :, GR:, :]


def join(k, v, r, heads, base):
    n = len(heads)
    return pl.pallas_call(
        functools.partial(join_kernel, heads, base),
        in_specs=[VM] * 5,
        out_specs=[VM] * 2,
        out_shape=[
            jax.ShapeDtypeStruct((n, 2, 2 * GR, HD), BF),
            jax.ShapeDtypeStruct((n, 2, GR, HD), BF),
        ],
        compiler_params=small(),
        cost_estimate=cost(0 if heads[0] == 0 else 3e10, 6 * 2 * GR * n * HD * 2),
        name="join",
    )(k, v, *r)


def attend_kernel(
    heads, base, win, near_, far_, own_, queries, upstream, r1, r2, r3,
    dq_, nearg_, farg_, owng_, q_ref, g_ref, s_ref, d_ref,
):
    me = lax.axis_index("head")

    def hidden(c, slot):
        return jnp.where(win[c, slot] >= 0, 0.0, 1e30).astype(F32)

    lane = lax.broadcasted_iota(jnp.int32, (1, 2 * GR), 1)

    def lanes(a, b):
        return jnp.where(lane < GR, a, b)

    one = jnp.full((1, GR), 1.0, F32)
    hides = (
        one * hidden(0, 2),
        lanes(hidden(0, 1), hidden(1, 2)),
        lanes(hidden(0, 0), hidden(1, 1)),
        lanes(0.0, hidden(1, 0)),
        one * 0.0,
    )

    def rows_of(i):
        return slice(i * GR, (i + 1) * GR)

    def combine(x, op):
        mid = op(op(x[1], x[2]), x[3])
        return jnp.concatenate([op(mid[:, :GR], x[0]), op(mid[:, GR:], x[4])], axis=1)

    def head(n, carry):
        near, far, own = near_.at[n], far_.at[n], own_.at[n]
        nearg, farg, owng = nearg_.at[n], farg_.at[n], owng_.at[n]
        q_ref[piece_rows(me), :] = queries[:, columns(me, heads[0] + n)]
        g_ref[piece_rows(me), :] = upstream[:, columns(me, heads[0] + n)]
        for d, r in ((1, r1), (3, r2), (2, r3)):
            rows = piece_rows(lax.rem(me + 4 - d, 4))
            q_ref[rows, :] = r[base + 2 * n]
            g_ref[rows, :] = r[base + 2 * n + 1]
        blocks = (
            (far, farg, 0, 0, 0, GR, hides[0]),
            (near, nearg, 0, 1, 0, 2 * GR, hides[1]),
            (near, nearg, 1, 2, 0, 2 * GR, hides[2]),
            (own, owng, 0, 3, 0, 2 * GR, hides[3]),
            (own, owng, 1, 4, GR, 2 * GR, hides[4]),
        )
        tops = []
        for ref, _, i, j, lo, hi, hide in blocks:
            s = dot(ref[0, rows_of(i), :], q_ref[lo:hi, :], NT)
            s_ref[rows_of(j), lo:hi] = s
            tops.append(jnp.max(s, axis=0, keepdims=True) * SCALE2 - hide)
        top = combine(tops, jnp.maximum)
        totals, deltas = [], []
        for ref, _, i, j, lo, hi, hide in blocks:
            dp = dot(ref[1, rows_of(i), :], g_ref[lo:hi, :], NT)
            e = jnp.exp2(s_ref[rows_of(j), lo:hi] * SCALE2 - (top[:, lo:hi] + hide))
            s_ref[rows_of(j), lo:hi] = e
            d_ref[rows_of(j), lo:hi] = dp
            totals.append(jnp.sum(e, axis=0, keepdims=True))
            deltas.append(jnp.sum(e * dp, axis=0, keepdims=True))
        inverse = 1.0 / combine(totals, jnp.add)
        delta = combine(deltas, jnp.add) * inverse
        column = jnp.transpose(jnp.broadcast_to(inverse, (HD, 2 * GR)))
        g = (g_ref[...].astype(F32) * column).astype(BF)
        q = (q_ref[...].astype(F32) * (column * SCALE)).astype(BF)
        dq = [None, None]
        for ref, out, i, j, lo, hi, hide in blocks:
            e = s_ref[rows_of(j), lo:hi]
            ds = (e * (d_ref[rows_of(j), lo:hi] - delta[:, lo:hi])).astype(BF)
            out[1, rows_of(i), :] = dot(e.astype(BF), g[lo:hi]).astype(out.dtype)
            out[0, rows_of(i), :] = dot(ds, q[lo:hi]).astype(out.dtype)
            part = dot(ref[0, rows_of(i), :], ds, TN)
            if lo == 0:
                dq[0] = part[:, :GR] if dq[0] is None else dq[0] + part[:, :GR]
            if hi == 2 * GR:
                dq[1] = part[:, -GR:] if dq[1] is None else dq[1] + part[:, -GR:]
        for i in range(2):
            factor = inverse[:, rows_of(i)] * SCALE
            dq_[n, rows_of(i), :] = (dq[i] * factor).T.astype(BF)
        return carry

    if len(heads) == 1:
        head(0, 0)
    else:
        lax.fori_loop(0, len(heads), head, 0)


def attend(window, near, far, own, queries, upstream, r, heads, base):
    n = len(heads)
    sd = jax.ShapeDtypeStruct
    return pl.pallas_call(
        functools.partial(attend_kernel, heads, base),
        in_specs=[pl.BlockSpec(memory_space=pltpu.SMEM)] + [VM] * 8,
        out_specs=[VM] * 4,
        out_shape=[
            sd((n, 2 * GR, HD), BF),
            sd((n, 2, 2 * GR, HD), BF),
            sd((n, 2, GR, HD), BF),
            sd((n, 2, 2 * GR, HD), F32),
        ],
        scratch_shapes=[
            pltpu.VMEM((2 * GR, HD), BF),
            pltpu.VMEM((2 * GR, HD), BF),
            pltpu.VMEM((5 * GR, 2 * GR), F32),
            pltpu.VMEM((5 * GR, 2 * GR), F32),
        ],
        compiler_params=pltpu.CompilerParams(vmem_limit_bytes=32 << 20),
        cost_estimate=cost(n * 5.5e9, n * 3e6),
        name="attend",
    )(window, near, far, own, queries, upstream, *r)


def settle_kernel(stage, *refs):
    me = lax.axis_index("head")
    outs = refs[-4:]
    refs = list(refs[:-4])
    u = 0
    for what, chunk in stage:
        if what == "dq":
            dq = refs.pop(0)
        else:
            owng, nearg, farg = refs.pop(0), refs.pop(0), refs.pop(0)
        for n in range(CHUNKS[chunk]):
            for d, out in zip((0, 1, 3, 2), outs):
                owner = lax.rem(me + d, 4)
                rows = piece_rows(owner)
                far_rows = piece_rows(lax.rem(owner, 2))
                if what == "dq":
                    out[u] = dq[n, rows, :]
                    continue
                for i in range(2):
                    late = jnp.where(owner >= 2, farg[n, i, far_rows, :].astype(F32), 0.0)
                    total = owng[n, i, rows, :] + nearg[n, i, rows, :].astype(F32) + late
                    out[u + i] = total.astype(BF)
            u += 1 if what == "dq" else 2


def settle(stage, operands):
    out = jax.ShapeDtypeStruct((len(out_units(stage)), PR, HD), BF)
    return pl.pallas_call(
        functools.partial(settle_kernel, stage),
        in_specs=[VM] * len(operands),
        out_specs=[VM] * 4,
        out_shape=[out] * 4,
        compiler_params=small(),
        cost_estimate=cost(0, 16 * len(out_units(stage)) * PR * HD * 2),
        name="settle",
    )(*operands)


def place_kernel(names, *refs):
    outs = dict(zip(names, refs[-len(names) :]))
    me = lax.axis_index("head")
    for c, stage in enumerate(OUT_STAGES[: len(refs) // 4]):
        for d, r in zip((0, 1, 3, 2), refs[4 * c : 4 * c + 4]):
            owner = lax.rem(me + 4 - d, 4)
            for u, (name, head) in enumerate(out_units(stage)):
                if name in names:
                    outs[name][:, columns(owner, head)] = r[u]


def place(names, pieces):
    out = jax.ShapeDtypeStruct((PR, 4 * HEADS_DEV * HD), BF)
    n = len(pieces)
    return pl.pallas_call(
        functools.partial(place_kernel, names),
        in_specs=[VM] * n,
        out_specs=[VM] * len(names),
        out_shape=[out] * len(names),
        compiler_params=small(),
        cost_estimate=cost(0, 6 * PR * 2560 * 2),
        name="place",
    )(*pieces)


def shift_all(pieces):
    a, b, c = pieces
    c = head_shift(c, 2)
    return head_shift(a, 1), head_shift(b, -1), c


def after(x, earlier):
    return lax.optimization_barrier((x, earlier))[0]


def local(queries, keys, values, upstream, window):
    args = {"q": queries, "k": keys, "v": values, "g": upstream}
    place_of = {}
    for i, stage in enumerate(IN_STAGES):
        base = 0
        for what, chunk in stage:
            place_of[what, chunk] = (i, base)
            base += 2 * CHUNKS[chunk]
    packed = [pack(args, stage) for stage in IN_STAGES]
    came = {}
    local_of = {}
    other = {}
    back = {}

    def send_in(i):
        came[i] = shift_all(packed[i])

    def join_chunk(c):
        i, base = place_of["kv", c]
        local_of[c] = join(keys, values, came[i], heads_of(c), base)

    def send_near(c):
        own, last = local_of[c]
        other[c] = tm_shift(own, 1), tm_shift(last, 2)

    def attend_chunk(c):
        i, base = place_of["qg", c]
        return attend(
            window, *other[c], local_of[c][0], queries, upstream, came[i], heads_of(c), base
        )

    def send_back(c):
        back[c] = tm_shift(grads[c][1], -1), tm_shift(grads[c][2], -2)

    grads = {}
    pieces = {}
    kept = {}

    def settle_stage(j):
        operands = []
        for what, c in OUT_STAGES[j]:
            operands += [grads[c][0]] if what == "dq" else [grads[c][3], *back[c]]
        own, *parts = settle(OUT_STAGES[j], operands)
        kept[j] = own
        return parts

    def send_out(j, parts):
        pieces[j] = [kept[j], *shift_all(parts)]

    send_in(0)
    packed[1] = [after(x, y) for x, y in zip(packed[1], came[0])]
    send_in(1)
    join_chunk(0)
    send_near(0)
    join_chunk(1)
    local_of[1] = after(local_of[1], other[0])
    send_near(1)
    packed[2] = after(packed[2], local_of[1])
    send_in(2)
    grads[0] = attend_chunk(0)
    came[2] = after(came[2], grads[0][0])
    send_back(0)
    grads[1] = attend_chunk(1)
    grads[1] = after(grads[1], back[0])
    parts0 = settle_stage(0)
    send_out(0, parts0)
    send_back(1)
    parts1 = settle_stage(1)
    parts1 = [after(x, y) for x, y in zip(parts1, pieces[0][1:])]
    send_out(1, parts1)
    (grad_q,) = place("q", pieces[0])
    grad_k, grad_v = place("kv", pieces[0] + pieces[1])
    return grad_q, grad_k, grad_v


def solution(mesh):
    rows = P(("tm", "head"), None)
    return jax.shard_map(
        local,
        mesh=mesh,
        in_specs=(rows, rows, rows, rows, P("tm", None)),
        out_specs=(rows, rows, rows),
        check_vma=False,
    )
```

```python
import functools
import math

import jax
import jax.numpy as jnp
from jax import lax
from jax.experimental import pallas as pl
from jax.experimental.pallas import tpu as pltpu
from jax.sharding import PartitionSpec as P

HD = 128
GR = 384
PR = 192
HEADS_DEV = 5
CHUNKS = (2, 3)
IN_STAGES = (
    (("kv", 0),),
    (("qg", 0), ("kv", 1)),
    (("qg", 1),),
)
OUT_STAGES = ((("dq", 0), ("dkv", 0), ("dq", 1)), (("dkv", 1),))
SCALE = 1.0 / math.sqrt(HD)
SCALE2 = SCALE * math.log2(math.e)
NT = (((1,), (1,)), ((), ()))
TN = (((0,), (0,)), ((), ()))
BF = jnp.bfloat16
F32 = jnp.float32
VM = pl.BlockSpec(memory_space=pltpu.VMEM)


def dot(a, b, dims=(((1,), (0,)), ((), ()))):
    return lax.dot_general(a, b, dims, preferred_element_type=F32)


def cost(flops, nbytes):
    return pl.CostEstimate(flops=int(flops * 1), bytes_accessed=int(nbytes * 1), transcendentals=0)


def head_shift(block, distance):
    n = lax.axis_size("head")
    return lax.ppermute(block, "head", [(i, (i + distance) % n) for i in range(n)])


def tm_shift(block, distance):
    devices = range(lax.axis_size("tm"))
    route = [(i - distance, i) for i in devices if i - distance in devices]
    return lax.ppermute(block, "tm", route)


def columns(owner, head):
    return pl.ds(pl.multiple_of((owner * HEADS_DEV + head) * HD, HD), HD)


def piece_rows(owner):
    return pl.ds(pl.multiple_of(owner * PR, 64), PR)


def heads_of(chunk):
    first = sum(CHUNKS[:chunk])
    return range(first, first + CHUNKS[chunk])


def in_units(stage):
    units = []
    for what, chunk in stage:
        for head in heads_of(chunk):
            units += [(what[0], head), (what[1], head)]
    return units


def out_units(stage):
    units = []
    for what, chunk in stage:
        for head in heads_of(chunk):
            units += [(o, head) for o in what[1:]]
    return units


def small():
    return pltpu.CompilerParams(vmem_limit_bytes=24 << 20)


def pack_kernel(units, names, *refs):
    me = lax.axis_index("head")
    srcs = dict(zip(names, refs))
    for d, out in zip((1, 3, 2), refs[len(names) :]):
        owner = lax.rem(me + d, 4)
        for u, (name, head) in enumerate(units):
            out[u] = srcs[name][:, columns(owner, head)]


def pack(args, stage):
    units = in_units(stage)
    names = sorted({name for name, _ in units})
    out = jax.ShapeDtypeStruct((len(units), PR, HD), BF)
    return pl.pallas_call(
        functools.partial(pack_kernel, units, names),
        in_specs=[VM] * len(names),
        out_specs=[VM] * 3,
        out_shape=[out] * 3,
        compiler_params=small(),
        cost_estimate=cost(0, 6 * len(units) * PR * HD * 2),
        name="pack",
    )(*[args[name] for name in names])


def join_kernel(heads, base, k, v, r1, r2, r3, own, last):
    me = lax.axis_index("head")
    for n, head in enumerate(heads):
        own[n, 0, piece_rows(me), :] = k[:, columns(me, head)]
        own[n, 1, piece_rows(me), :] = v[:, columns(me, head)]
        for d, r in ((1, r1), (3, r2), (2, r3)):
            rows = piece_rows(lax.rem(me + 4 - d, 4))
            own[n, 0, rows, :] = r[base + 2 * n]
            own[n, 1, rows, :] = r[base + 2 * n + 1]
    last[...] = own[:, :, GR:, :]


def join(k, v, r, heads, base):
    n = len(heads)
    return pl.pallas_call(
        functools.partial(join_kernel, heads, base),
        in_specs=[VM] * 5,
        out_specs=[VM] * 2,
        out_shape=[
            jax.ShapeDtypeStruct((n, 2, 2 * GR, HD), BF),
            jax.ShapeDtypeStruct((n, 2, GR, HD), BF),
        ],
        compiler_params=small(),
        cost_estimate=cost(0 if heads[0] == 0 else 3e10, 6 * 2 * GR * n * HD * 2),
        name="join",
    )(k, v, *r)


def attend_kernel(
    heads, base, win, near_, far_, own_, queries, upstream, r1, r2, r3,
    dq_, nearg_, farg_, owng_, q_ref, g_ref, s_ref, d_ref,
):
    me = lax.axis_index("head")

    def hidden(c, slot):
        return jnp.where(win[c, slot] >= 0, 0.0, 1e30).astype(F32)

    lane = lax.broadcasted_iota(jnp.int32, (1, 2 * GR), 1)

    def lanes(a, b):
        return jnp.where(lane < GR, a, b)

    one = jnp.full((1, GR), 1.0, F32)
    hides = (
        one * hidden(0, 2),
        lanes(hidden(0, 1), hidden(1, 2)),
        lanes(hidden(0, 0), hidden(1, 1)),
        lanes(0.0, hidden(1, 0)),
        one * 0.0,
    )

    def rows_of(i):
        return slice(i * GR, (i + 1) * GR)

    def combine(x, op):
        mid = op(op(x[1], x[2]), x[3])
        return jnp.concatenate([op(mid[:, :GR], x[0]), op(mid[:, GR:], x[4])], axis=1)

    def head(n, carry):
        near, far, own = near_.at[n], far_.at[n], own_.at[n]
        nearg, farg, owng = nearg_.at[n], farg_.at[n], owng_.at[n]
        q_ref[piece_rows(me), :] = queries[:, columns(me, heads[0] + n)]
        g_ref[piece_rows(me), :] = upstream[:, columns(me, heads[0] + n)]
        for d, r in ((1, r1), (3, r2), (2, r3)):
            rows = piece_rows(lax.rem(me + 4 - d, 4))
            q_ref[rows, :] = r[base + 2 * n]
            g_ref[rows, :] = r[base + 2 * n + 1]
        blocks = (
            (far, farg, 0, 0, 0, GR, hides[0]),
            (near, nearg, 0, 1, 0, 2 * GR, hides[1]),
            (near, nearg, 1, 2, 0, 2 * GR, hides[2]),
            (own, owng, 0, 3, 0, 2 * GR, hides[3]),
            (own, owng, 1, 4, GR, 2 * GR, hides[4]),
        )
        tops = []
        for ref, _, i, j, lo, hi, hide in blocks:
            s = dot(ref[0, rows_of(i), :], q_ref[lo:hi, :], NT)
            s_ref[rows_of(j), lo:hi] = s
            tops.append(jnp.max(s, axis=0, keepdims=True) * SCALE2 - hide)
        top = combine(tops, jnp.maximum)
        totals, deltas = [], []
        for ref, _, i, j, lo, hi, hide in blocks:
            dp = dot(ref[1, rows_of(i), :], g_ref[lo:hi, :], NT)
            e = jnp.exp2(s_ref[rows_of(j), lo:hi] * SCALE2 - (top[:, lo:hi] + hide))
            s_ref[rows_of(j), lo:hi] = e
            d_ref[rows_of(j), lo:hi] = dp
            totals.append(jnp.sum(e, axis=0, keepdims=True))
            deltas.append(jnp.sum(e * dp, axis=0, keepdims=True))
        inverse = 1.0 / combine(totals, jnp.add)
        delta = combine(deltas, jnp.add) * inverse
        column = jnp.transpose(jnp.broadcast_to(inverse, (HD, 2 * GR)))
        g = (g_ref[...].astype(F32) * column).astype(BF)
        q = (q_ref[...].astype(F32) * (column * SCALE)).astype(BF)
        dq = [None, None]
        for ref, out, i, j, lo, hi, hide in blocks:
            e = s_ref[rows_of(j), lo:hi]
            ds = (e * (d_ref[rows_of(j), lo:hi] - delta[:, lo:hi])).astype(BF)
            out[1, rows_of(i), :] = dot(e.astype(BF), g[lo:hi]).astype(out.dtype)
            out[0, rows_of(i), :] = dot(ds, q[lo:hi]).astype(out.dtype)
            part = dot(ref[0, rows_of(i), :], ds, TN)
            if lo == 0:
                dq[0] = part[:, :GR] if dq[0] is None else dq[0] + part[:, :GR]
            if hi == 2 * GR:
                dq[1] = part[:, -GR:] if dq[1] is None else dq[1] + part[:, -GR:]
        for i in range(2):
            factor = inverse[:, rows_of(i)] * SCALE
            dq_[n, rows_of(i), :] = (dq[i] * factor).T.astype(BF)
        return carry

    if len(heads) == 1:
        head(0, 0)
    else:
        lax.fori_loop(0, len(heads), head, 0)


def attend(window, near, far, own, queries, upstream, r, heads, base):
    n = len(heads)
    sd = jax.ShapeDtypeStruct
    return pl.pallas_call(
        functools.partial(attend_kernel, heads, base),
        in_specs=[pl.BlockSpec(memory_space=pltpu.SMEM)] + [VM] * 8,
        out_specs=[VM] * 4,
        out_shape=[
            sd((n, 2 * GR, HD), BF),
            sd((n, 2, 2 * GR, HD), BF),
            sd((n, 2, GR, HD), BF),
            sd((n, 2, 2 * GR, HD), F32),
        ],
        scratch_shapes=[
            pltpu.VMEM((2 * GR, HD), BF),
            pltpu.VMEM((2 * GR, HD), BF),
            pltpu.VMEM((5 * GR, 2 * GR), F32),
            pltpu.VMEM((5 * GR, 2 * GR), F32),
        ],
        compiler_params=pltpu.CompilerParams(vmem_limit_bytes=32 << 20),
        cost_estimate=cost(n * 5.5e9, n * 3e6),
        name="attend",
    )(window, near, far, own, queries, upstream, *r)


def settle_kernel(stage, *refs):
    me = lax.axis_index("head")
    outs = refs[-4:]
    refs = list(refs[:-4])
    u = 0
    for what, chunk in stage:
        if what == "dq":
            dq = refs.pop(0)
        else:
            owng, nearg, farg = refs.pop(0), refs.pop(0), refs.pop(0)
        for n in range(CHUNKS[chunk]):
            for d, out in zip((0, 1, 3, 2), outs):
                owner = lax.rem(me + d, 4)
                rows = piece_rows(owner)
                far_rows = piece_rows(lax.rem(owner, 2))
                if what == "dq":
                    out[u] = dq[n, rows, :]
                    continue
                for i in range(2):
                    late = jnp.where(owner >= 2, farg[n, i, far_rows, :].astype(F32), 0.0)
                    total = owng[n, i, rows, :] + nearg[n, i, rows, :].astype(F32) + late
                    out[u + i] = total.astype(BF)
            u += 1 if what == "dq" else 2


def settle(stage, operands):
    out = jax.ShapeDtypeStruct((len(out_units(stage)), PR, HD), BF)
    return pl.pallas_call(
        functools.partial(settle_kernel, stage),
        in_specs=[VM] * len(operands),
        out_specs=[VM] * 4,
        out_shape=[out] * 4,
        compiler_params=small(),
        cost_estimate=cost(0, 16 * len(out_units(stage)) * PR * HD * 2),
        name="settle",
    )(*operands)


def place_kernel(names, *refs):
    outs = dict(zip(names, refs[-len(names) :]))
    me = lax.axis_index("head")
    for c, stage in enumerate(OUT_STAGES[: len(refs) // 4]):
        for d, r in zip((0, 1, 3, 2), refs[4 * c : 4 * c + 4]):
            owner = lax.rem(me + 4 - d, 4)
            for u, (name, head) in enumerate(out_units(stage)):
                if name in names:
                    outs[name][:, columns(owner, head)] = r[u]


def place(names, pieces):
    out = jax.ShapeDtypeStruct((PR, 4 * HEADS_DEV * HD), BF)
    n = len(pieces)
    return pl.pallas_call(
        functools.partial(place_kernel, names),
        in_specs=[VM] * n,
        out_specs=[VM] * len(names),
        out_shape=[out] * len(names),
        compiler_params=small(),
        cost_estimate=cost(0, 6 * PR * 2560 * 2),
        name="place",
    )(*pieces)


def shift_all(pieces):
    a, b, c = pieces
    c = head_shift(c, 2)
    return head_shift(a, 1), head_shift(b, -1), c


def after(x, earlier):
    return lax.optimization_barrier((x, earlier))[0]


def local(queries, keys, values, upstream, window):
    args = {"q": queries, "k": keys, "v": values, "g": upstream}
    place_of = {}
    for i, stage in enumerate(IN_STAGES):
        base = 0
        for what, chunk in stage:
            place_of[what, chunk] = (i, base)
            base += 2 * CHUNKS[chunk]
    packed = [pack(args, stage) for stage in IN_STAGES]
    came = {}
    local_of = {}
    other = {}
    back = {}

    def send_in(i):
        came[i] = shift_all(packed[i])

    def join_chunk(c):
        i, base = place_of["kv", c]
        local_of[c] = join(keys, values, came[i], heads_of(c), base)

    def send_near(c):
        own, last = local_of[c]
        other[c] = tm_shift(own, 1), tm_shift(last, 2)

    def attend_chunk(c):
        i, base = place_of["qg", c]
        return attend(
            window, *other[c], local_of[c][0], queries, upstream, came[i], heads_of(c), base
        )

    def send_back(c):
        back[c] = tm_shift(grads[c][1], -1), tm_shift(grads[c][2], -2)

    grads = {}
    pieces = {}
    kept = {}

    def settle_stage(j):
        operands = []
        for what, c in OUT_STAGES[j]:
            operands += [grads[c][0]] if what == "dq" else [grads[c][3], *back[c]]
        own, *parts = settle(OUT_STAGES[j], operands)
        kept[j] = own
        return parts

    def send_out(j, parts):
        pieces[j] = [kept[j], *shift_all(parts)]

    send_in(0)
    packed[1] = [after(x, y) for x, y in zip(packed[1], came[0])]
    send_in(1)
    join_chunk(0)
    send_near(0)
    join_chunk(1)
    local_of[1] = after(local_of[1], other[0])
    send_near(1)
    packed[2] = after(packed[2], local_of[1])
    send_in(2)
    grads[0] = attend_chunk(0)
    came[2] = after(came[2], grads[0][0])
    send_back(0)
    grads[1] = attend_chunk(1)
    grads[1] = after(grads[1], back[0])
    parts0 = settle_stage(0)
    send_out(0, parts0)
    send_back(1)
    parts1 = settle_stage(1)
    send_out(1, parts1)
    (grad_q,) = place("q", pieces[0])
    grad_k, grad_v = place("kv", pieces[0] + pieces[1])
    return grad_q, grad_k, grad_v


def solution(mesh):
    rows = P(("tm", "head"), None)
    return jax.shard_map(
        local,
        mesh=mesh,
        in_specs=(rows, rows, rows, rows, P("tm", None)),
        out_specs=(rows, rows, rows),
        check_vma=False,
    )
```

```python
import functools
import math

import jax
import jax.numpy as jnp
from jax import lax
from jax.experimental import pallas as pl
from jax.experimental.pallas import tpu as pltpu
from jax.sharding import PartitionSpec as P

HD = 128
GR = 384
PR = 192
HEADS_DEV = 5
CHUNKS = (2, 3)
IN_STAGES = (
    (("kv", 0),),
    (("qg", 0), ("kv", 1)),
    (("qg", 1),),
)
OUT_STAGES = ((("dq", 0), ("dkv", 0), ("dq", 1)), (("dkv", 1),))
SCALE = 1.0 / math.sqrt(HD)
SCALE2 = SCALE * math.log2(math.e)
NT = (((1,), (1,)), ((), ()))
TN = (((0,), (0,)), ((), ()))
BF = jnp.bfloat16
F32 = jnp.float32
VM = pl.BlockSpec(memory_space=pltpu.VMEM)


def dot(a, b, dims=(((1,), (0,)), ((), ()))):
    return lax.dot_general(a, b, dims, preferred_element_type=F32)


def cost(flops, nbytes):
    return pl.CostEstimate(flops=int(flops * 1), bytes_accessed=int(nbytes * 1), transcendentals=0)


def head_shift(block, distance):
    n = lax.axis_size("head")
    return lax.ppermute(block, "head", [(i, (i + distance) % n) for i in range(n)])


def tm_shift(block, distance):
    devices = range(lax.axis_size("tm"))
    route = [(i - distance, i) for i in devices if i - distance in devices]
    return lax.ppermute(block, "tm", route)


def columns(owner, head):
    return pl.ds(pl.multiple_of((owner * HEADS_DEV + head) * HD, HD), HD)


def piece_rows(owner):
    return pl.ds(pl.multiple_of(owner * PR, 64), PR)


def heads_of(chunk):
    first = sum(CHUNKS[:chunk])
    return range(first, first + CHUNKS[chunk])


def in_units(stage):
    units = []
    for what, chunk in stage:
        for head in heads_of(chunk):
            units += [(what[0], head), (what[1], head)]
    return units


def out_units(stage):
    units = []
    for what, chunk in stage:
        for head in heads_of(chunk):
            units += [(o, head) for o in what[1:]]
    return units


def small():
    return pltpu.CompilerParams(vmem_limit_bytes=24 << 20)


def pack_kernel(units, names, *refs):
    me = lax.axis_index("head")
    srcs = dict(zip(names, refs))
    for d, out in zip((1, 3, 2), refs[len(names) :]):
        owner = lax.rem(me + d, 4)
        for u, (name, head) in enumerate(units):
            out[u] = srcs[name][:, columns(owner, head)]


def pack(args, stage):
    units = in_units(stage)
    names = sorted({name for name, _ in units})
    out = jax.ShapeDtypeStruct((len(units), PR, HD), BF)
    return pl.pallas_call(
        functools.partial(pack_kernel, units, names),
        in_specs=[VM] * len(names),
        out_specs=[VM] * 3,
        out_shape=[out] * 3,
        compiler_params=small(),
        cost_estimate=cost(0, 6 * len(units) * PR * HD * 2),
        name="pack",
    )(*[args[name] for name in names])


def join_kernel(heads, base, k, v, r1, r2, r3, own, last):
    me = lax.axis_index("head")
    for n, head in enumerate(heads):
        own[n, 0, piece_rows(me), :] = k[:, columns(me, head)]
        own[n, 1, piece_rows(me), :] = v[:, columns(me, head)]
        for d, r in ((1, r1), (3, r2), (2, r3)):
            rows = piece_rows(lax.rem(me + 4 - d, 4))
            own[n, 0, rows, :] = r[base + 2 * n]
            own[n, 1, rows, :] = r[base + 2 * n + 1]
    last[...] = own[:, :, GR:, :]


def join(k, v, r, heads, base):
    n = len(heads)
    return pl.pallas_call(
        functools.partial(join_kernel, heads, base),
        in_specs=[VM] * 5,
        out_specs=[VM] * 2,
        out_shape=[
            jax.ShapeDtypeStruct((n, 2, 2 * GR, HD), BF),
            jax.ShapeDtypeStruct((n, 2, GR, HD), BF),
        ],
        compiler_params=small(),
        cost_estimate=cost(0 if heads[0] == 0 else 3e10, 6 * 2 * GR * n * HD * 2),
        name="join",
    )(k, v, *r)


def attend_kernel(
    heads, base, win, near_, far_, own_, queries, upstream, r1, r2, r3,
    dq_, nearg_, farg_, owng_, q_two, g_two, s_two, d_two,
):
    me = lax.axis_index("head")

    def hidden(c, slot):
        return jnp.where(win[c, slot] >= 0, 0.0, 1e30).astype(F32)

    lane = lax.broadcasted_iota(jnp.int32, (1, 2 * GR), 1)

    def lanes(a, b):
        return jnp.where(lane < GR, a, b)

    one = jnp.full((1, GR), 1.0, F32)
    hides = (
        one * hidden(0, 2),
        lanes(hidden(0, 1), hidden(1, 2)),
        lanes(hidden(0, 0), hidden(1, 1)),
        lanes(0.0, hidden(1, 0)),
        one * 0.0,
    )

    def rows_of(i):
        return slice(i * GR, (i + 1) * GR)

    def combine(x, op):
        mid = op(op(x[1], x[2]), x[3])
        return jnp.concatenate([op(mid[:, :GR], x[0]), op(mid[:, GR:], x[4])], axis=1)

    def head(n):
        q_ref, g_ref, s_ref, d_ref = [x.at[n % 2] for x in (q_two, g_two, s_two, d_two)]
        near, far, own = near_.at[n], far_.at[n], own_.at[n]
        nearg, farg, owng = nearg_.at[n], farg_.at[n], owng_.at[n]
        q_ref[piece_rows(me), :] = queries[:, columns(me, heads[0] + n)]
        g_ref[piece_rows(me), :] = upstream[:, columns(me, heads[0] + n)]
        for d, r in ((1, r1), (3, r2), (2, r3)):
            rows = piece_rows(lax.rem(me + 4 - d, 4))
            q_ref[rows, :] = r[base + 2 * n]
            g_ref[rows, :] = r[base + 2 * n + 1]
        blocks = (
            (far, farg, 0, 0, 0, GR, hides[0]),
            (near, nearg, 0, 1, 0, 2 * GR, hides[1]),
            (near, nearg, 1, 2, 0, 2 * GR, hides[2]),
            (own, owng, 0, 3, 0, 2 * GR, hides[3]),
            (own, owng, 1, 4, GR, 2 * GR, hides[4]),
        )
        tops = []
        for ref, _, i, j, lo, hi, hide in blocks:
            s = dot(ref[0, rows_of(i), :], q_ref[lo:hi, :], NT)
            s_ref[rows_of(j), lo:hi] = s
            tops.append(jnp.max(s, axis=0, keepdims=True) * SCALE2 - hide)
        top = combine(tops, jnp.maximum)
        totals, deltas = [], []
        for ref, _, i, j, lo, hi, hide in blocks:
            dp = dot(ref[1, rows_of(i), :], g_ref[lo:hi, :], NT)
            e = jnp.exp2(s_ref[rows_of(j), lo:hi] * SCALE2 - (top[:, lo:hi] + hide))
            s_ref[rows_of(j), lo:hi] = e
            d_ref[rows_of(j), lo:hi] = dp
            totals.append(jnp.sum(e, axis=0, keepdims=True))
            deltas.append(jnp.sum(e * dp, axis=0, keepdims=True))
        inverse = 1.0 / combine(totals, jnp.add)
        delta = combine(deltas, jnp.add) * inverse
        column = jnp.transpose(jnp.broadcast_to(inverse, (HD, 2 * GR)))
        g = (g_ref[...].astype(F32) * column).astype(BF)
        q = (q_ref[...].astype(F32) * (column * SCALE)).astype(BF)
        dq = [None, None]
        for ref, out, i, j, lo, hi, hide in blocks:
            e = s_ref[rows_of(j), lo:hi]
            ds = (e * (d_ref[rows_of(j), lo:hi] - delta[:, lo:hi])).astype(BF)
            out[1, rows_of(i), :] = dot(e.astype(BF), g[lo:hi]).astype(out.dtype)
            out[0, rows_of(i), :] = dot(ds, q[lo:hi]).astype(out.dtype)
            part = dot(ref[0, rows_of(i), :], ds, TN)
            if lo == 0:
                dq[0] = part[:, :GR] if dq[0] is None else dq[0] + part[:, :GR]
            if hi == 2 * GR:
                dq[1] = part[:, -GR:] if dq[1] is None else dq[1] + part[:, -GR:]
        for i in range(2):
            factor = inverse[:, rows_of(i)] * SCALE
            dq_[n, rows_of(i), :] = (dq[i] * factor).T.astype(BF)

    for n in range(len(heads)):
        head(n)


def attend(window, near, far, own, queries, upstream, r, heads, base):
    n = len(heads)
    sd = jax.ShapeDtypeStruct
    return pl.pallas_call(
        functools.partial(attend_kernel, heads, base),
        in_specs=[pl.BlockSpec(memory_space=pltpu.SMEM)] + [VM] * 8,
        out_specs=[VM] * 4,
        out_shape=[
            sd((n, 2 * GR, HD), BF),
            sd((n, 2, 2 * GR, HD), BF),
            sd((n, 2, GR, HD), BF),
            sd((n, 2, 2 * GR, HD), F32),
        ],
        scratch_shapes=[
            pltpu.VMEM((2, 2 * GR, HD), BF),
            pltpu.VMEM((2, 2 * GR, HD), BF),
            pltpu.VMEM((2, 5 * GR, 2 * GR), F32),
            pltpu.VMEM((2, 5 * GR, 2 * GR), F32),
        ],
        compiler_params=pltpu.CompilerParams(vmem_limit_bytes=32 << 20),
        cost_estimate=cost(n * 5.5e9, n * 3e6),
        name="attend",
    )(window, near, far, own, queries, upstream, *r)


def settle_kernel(stage, *refs):
    me = lax.axis_index("head")
    outs = refs[-4:]
    refs = list(refs[:-4])
    u = 0
    for what, chunk in stage:
        if what == "dq":
            dq = refs.pop(0)
        else:
            owng, nearg, farg = refs.pop(0), refs.pop(0), refs.pop(0)
        for n in range(CHUNKS[chunk]):
            for d, out in zip((0, 1, 3, 2), outs):
                owner = lax.rem(me + d, 4)
                rows = piece_rows(owner)
                far_rows = piece_rows(lax.rem(owner, 2))
                if what == "dq":
                    out[u] = dq[n, rows, :]
                    continue
                for i in range(2):
                    late = jnp.where(owner >= 2, farg[n, i, far_rows, :].astype(F32), 0.0)
                    total = owng[n, i, rows, :] + nearg[n, i, rows, :].astype(F32) + late
                    out[u + i] = total.astype(BF)
            u += 1 if what == "dq" else 2


def settle(stage, operands):
    out = jax.ShapeDtypeStruct((len(out_units(stage)), PR, HD), BF)
    return pl.pallas_call(
        functools.partial(settle_kernel, stage),
        in_specs=[VM] * len(operands),
        out_specs=[VM] * 4,
        out_shape=[out] * 4,
        compiler_params=small(),
        cost_estimate=cost(0, 16 * len(out_units(stage)) * PR * HD * 2),
        name="settle",
    )(*operands)


def place_kernel(names, *refs):
    outs = dict(zip(names, refs[-len(names) :]))
    me = lax.axis_index("head")
    for c, stage in enumerate(OUT_STAGES[: len(refs) // 4]):
        for d, r in zip((0, 1, 3, 2), refs[4 * c : 4 * c + 4]):
            owner = lax.rem(me + 4 - d, 4)
            for u, (name, head) in enumerate(out_units(stage)):
                if name in names:
                    outs[name][:, columns(owner, head)] = r[u]


def place(names, pieces):
    out = jax.ShapeDtypeStruct((PR, 4 * HEADS_DEV * HD), BF)
    n = len(pieces)
    return pl.pallas_call(
        functools.partial(place_kernel, names),
        in_specs=[VM] * n,
        out_specs=[VM] * len(names),
        out_shape=[out] * len(names),
        compiler_params=small(),
        cost_estimate=cost(0, 6 * PR * 2560 * 2),
        name="place",
    )(*pieces)


def shift_all(pieces):
    a, b, c = pieces
    c = head_shift(c, 2)
    return head_shift(a, 1), head_shift(b, -1), c


def after(x, earlier):
    return lax.optimization_barrier((x, earlier))[0]


def local(queries, keys, values, upstream, window):
    args = {"q": queries, "k": keys, "v": values, "g": upstream}
    place_of = {}
    for i, stage in enumerate(IN_STAGES):
        base = 0
        for what, chunk in stage:
            place_of[what, chunk] = (i, base)
            base += 2 * CHUNKS[chunk]
    packed = [pack(args, stage) for stage in IN_STAGES]
    came = {}
    local_of = {}
    other = {}
    back = {}

    def send_in(i):
        came[i] = shift_all(packed[i])

    def join_chunk(c):
        i, base = place_of["kv", c]
        local_of[c] = join(keys, values, came[i], heads_of(c), base)

    def send_near(c):
        own, last = local_of[c]
        other[c] = tm_shift(own, 1), tm_shift(last, 2)

    def attend_chunk(c):
        i, base = place_of["qg", c]
        return attend(
            window, *other[c], local_of[c][0], queries, upstream, came[i], heads_of(c), base
        )

    def send_back(c):
        back[c] = tm_shift(grads[c][1], -1), tm_shift(grads[c][2], -2)

    grads = {}
    pieces = {}
    kept = {}

    def settle_stage(j):
        operands = []
        for what, c in OUT_STAGES[j]:
            operands += [grads[c][0]] if what == "dq" else [grads[c][3], *back[c]]
        own, *parts = settle(OUT_STAGES[j], operands)
        kept[j] = own
        return parts

    def send_out(j, parts):
        pieces[j] = [kept[j], *shift_all(parts)]

    send_in(0)
    packed[1] = [after(x, y) for x, y in zip(packed[1], came[0])]
    send_in(1)
    join_chunk(0)
    send_near(0)
    join_chunk(1)
    local_of[1] = after(local_of[1], other[0])
    send_near(1)
    packed[2] = after(packed[2], local_of[1])
    send_in(2)
    grads[0] = attend_chunk(0)
    came[2] = after(came[2], grads[0][0])
    send_back(0)
    grads[1] = attend_chunk(1)
    grads[1] = after(grads[1], back[0])
    parts0 = settle_stage(0)
    send_out(0, parts0)
    send_back(1)
    parts1 = settle_stage(1)
    send_out(1, parts1)
    (grad_q,) = place("q", pieces[0])
    grad_k, grad_v = place("kv", pieces[0] + pieces[1])
    return grad_q, grad_k, grad_v


def solution(mesh):
    rows = P(("tm", "head"), None)
    return jax.shard_map(
        local,
        mesh=mesh,
        in_specs=(rows, rows, rows, rows, P("tm", None)),
        out_specs=(rows, rows, rows),
        check_vma=False,
    )
```
